32 devices in a mesh: req: 8 (over z, y), tp: 4 (over x, core).
Axes of the slice: x: 2, y: 2, z: 4, core: 2. Of those that a mesh axis runs over, the one named last changes fastest.
Arguments:
- queries: bfloat16 [4096, 7168], P('req', 'tp')
- keys_new: bfloat16 [4096, 7168], P('req', 'tp')
- values_new: bfloat16 [4096, 7168], P('req', 'tp'), may hold values from -6 to 6
- cache_keys: bfloat16 [16, 1024, 7168], P('req', None, 'tp'), may hold values from -6 to 6
- cache_values: bfloat16 [16, 1024, 7168], P('req', None, 'tp'), may hold values from -6 to 6
- out_proj: bfloat16 [7168, 3584], P('tp'), may hold values from -0.0625 to 0.0625
- req_lengths: int32 [8, 4], P('req'), may hold values from 1 to 415, as said below
- cache_owner: int32 [8, 2], P('req'), may hold values from 0 to 7, as said below
- cache_slot: int32 [8, 2], P('req'), may hold values from 0 to 1
- prior_len: int32 [8, 2], P('req'), may hold values from 1 to 1024, as said below
Outputs:
- mixed: bfloat16 [4096, 3584], P(('req', 'tp'))
- new_keys: bfloat16 [16, 192, 7168], P('req', None, 'tp')
- new_values: bfloat16 [16, 192, 7168], P('req', None, 'tp')
The draws below stay inside these ranges and needn't reach their ends.
Inputs may be any that keep to these rules, and one draw needn't show every extreme that they name: `req_lengths`: each row sums to 512; each continuing request has at most 192 new tokens, and some continuing request has exactly 192; continuing requests have at least 48 new tokens; some request has exactly 415. `cache_owner`: A continuing request's owner is the req index just before or just after its own, counted around the axis (index 0 follows index 7); the two continuing requests of one index have different owners; every cache slot of every index is used by exactly one continuing request. `prior_len`: some continuing request has exactly 1024 prior tokens.
All inputs are finite; a program needn't handle non-finite values.
Results may differ from the reference program's by a relative error of at most 0.014.
Values may be sent and summed in bfloat16 or wider, within the bound.
A program may use at most 128 MiB of HBM per device.

```python
import math
import jax
import jax.numpy as jnp
from jax import lax

D = 3584
HEADS = 32
HD = 224
ATT = 7168
T_DEV = 512
SLOTS = 2
NEWCAP = 192
PMAX = 1024
TOKENS = 4096
N_REQ = 8


def shared_query_key(key):
    key_base = jax.random.normal(jax.random.fold_in(key, 11), (TOKENS, HEADS * HD), jnp.float32)
    query_out = jax.random.normal(jax.random.fold_in(key, 12), (TOKENS, HEADS * HD), jnp.float32)
    keys_out = key_base
    return (query_out, keys_out)


def draw_queries(key, part):
    return shared_query_key(key)[0].astype(jnp.bfloat16)


def draw_keys_new(key, part):
    return shared_query_key(key)[1].astype(jnp.bfloat16)


def draw_req_lengths(key, part):
    continuing = jax.random.randint(jax.random.fold_in(key, 31), (N_REQ, SLOTS), NEWCAP // 4, NEWCAP + 1)
    chosen_device = jax.random.randint(jax.random.fold_in(key, 32), (), 0, N_REQ)
    chosen_slot = jax.random.randint(jax.random.fold_in(key, 33), (), 0, SLOTS)
    longest_device = (chosen_device + 1) % N_REQ
    grid_rows = jnp.arange(N_REQ)[:, None]
    grid_cols = jnp.arange(SLOTS)[None, :]
    continuing = jnp.where((grid_rows == chosen_device) & (grid_cols == chosen_slot), NEWCAP, continuing)
    continuing = jnp.where(grid_rows == longest_device, NEWCAP // 4, continuing)
    remaining = T_DEV - jnp.sum(continuing, axis=1)
    first_part = jax.random.randint(jax.random.fold_in(key, 34), (N_REQ,), 1, remaining)
    first_part = jnp.where(jnp.arange(N_REQ) == longest_device, remaining - 1, first_part)
    second_part = remaining - first_part
    return jnp.concatenate([continuing, first_part[:, None], second_part[:, None]], axis=1).astype(jnp.int32)


def owner_and_slot(key):
    device = jnp.arange(N_REQ)
    right_first = jax.random.randint(jax.random.fold_in(key, 41), (N_REQ,), 0, 2)
    owner_bit = jax.random.randint(jax.random.fold_in(key, 43), (N_REQ,), 0, 2)
    right_owner = (device + 1) % N_REQ
    left_owner = (device + N_REQ - 1) % N_REQ
    right_slot = owner_bit[right_owner]
    left_slot = 1 - owner_bit[left_owner]
    owner_first = jnp.where(right_first == 1, right_owner, left_owner)
    owner_second = jnp.where(right_first == 1, left_owner, right_owner)
    slot_first = jnp.where(right_first == 1, right_slot, left_slot)
    slot_second = jnp.where(right_first == 1, left_slot, right_slot)
    owners = jnp.stack([owner_first, owner_second], axis=1).astype(jnp.int32)
    slot_numbers = jnp.stack([slot_first, slot_second], axis=1).astype(jnp.int32)
    return (owners, slot_numbers)


def draw_cache_owner(key, part):
    return owner_and_slot(key)[0]


def draw_cache_slot(key, part):
    return owner_and_slot(key)[1]


def draw_prior_len(key, part):
    drawn = jax.random.randint(jax.random.fold_in(key, 51), (N_REQ, SLOTS), 1, PMAX + 1)
    chosen_device = jax.random.randint(jax.random.fold_in(key, 52), (), 0, N_REQ)
    chosen_slot = jax.random.randint(jax.random.fold_in(key, 53), (), 0, SLOTS)
    grid_rows = jnp.arange(N_REQ)[:, None]
    grid_cols = jnp.arange(SLOTS)[None, :]
    return jnp.where((grid_rows == chosen_device) & (grid_cols == chosen_slot), PMAX, drawn).astype(jnp.int32)


def level_of(stream_key, shape, split, smallest, top_value):
    level, own = 1.0, jax.random.fold_in(stream_key, 6)
    for position, shards_of in split:
        heights = jnp.exp(jax.random.uniform(jax.random.fold_in(own, position), (shards_of,), jnp.float32, smallest / len(split), top_value / len(split)))
        level = level * jnp.repeat(heights, shape[position] // shards_of).reshape([-1 if axis == position else 1 for axis in range(len(shape))])
    return level


def bell_draw(own_key, dims, spread, bound, split=(), kind=jnp.bfloat16):
    values = jax.random.normal(own_key, dims, jnp.float32) * spread
    if len(split) > 0:
        values = level_of(own_key, dims, split, -0.22, 0.18) * values
    return jnp.clip(values, min=-bound, max=bound).astype(kind)


def setup_inputs(seed: int = 0) -> dict:
    arg_keys = jax.random.split(jax.random.key(seed), 11)
    queries = draw_queries(jax.random.fold_in(arg_keys[10], 71), 0)
    keys_new = draw_keys_new(jax.random.fold_in(arg_keys[10], 71), 0)
    values_new = bell_draw(arg_keys[2], (TOKENS, ATT), 1.0, 6.0, ((0, 8), (1, 4)))
    cache_keys = bell_draw(arg_keys[3], (N_REQ * SLOTS, PMAX, ATT), 1.0, 6.0, ((0, 8), (2, 4)))
    cache_values = bell_draw(arg_keys[4], (N_REQ * SLOTS, PMAX, ATT), 1.0, 6.0, ((0, 8), (2, 4)))
    out_proj = bell_draw(arg_keys[5], (ATT, D), ATT ** -0.5, 0.0625, ((0, 4),))
    req_lengths = draw_req_lengths(jax.random.fold_in(arg_keys[10], 71), 0)
    cache_owner = draw_cache_owner(jax.random.fold_in(arg_keys[10], 71), 0)
    cache_slot = draw_cache_slot(jax.random.fold_in(arg_keys[10], 71), 0)
    prior_len = draw_prior_len(jax.random.fold_in(arg_keys[10], 71), 0)
    return dict(queries=queries, keys_new=keys_new, values_new=values_new, cache_keys=cache_keys, cache_values=cache_values, out_proj=out_proj, req_lengths=req_lengths, cache_owner=cache_owner, cache_slot=cache_slot, prior_len=prior_len)


def reference(queries, keys_new, values_new, cache_keys, cache_values, out_proj, req_lengths, cache_owner, cache_slot, prior_len):
    score_scale = 1.0 / math.sqrt(HD)
    positions = jnp.arange(T_DEV, dtype=jnp.int32)
    row_marks = jnp.arange(NEWCAP, dtype=jnp.int32)
    slot_of = jnp.repeat(jnp.arange(SLOTS, dtype=jnp.int32), PMAX)
    row_in_slot = jnp.tile(jnp.arange(PMAX, dtype=jnp.int32), SLOTS)

    def one_block(b):
        req_lens = req_lengths[b]
        req_ends = jnp.cumsum(req_lens).astype(jnp.int32)
        starts = (req_ends - req_lens).astype(jnp.int32)
        segment = lax.optimization_barrier(jnp.sum((positions[:, None] >= req_ends[None, :]).astype(jnp.int32), axis=1))
        first_row = (b * T_DEV).astype(jnp.int32)
        query_block = lax.dynamic_slice_in_dim(queries, first_row, T_DEV, 0)
        key_block = lax.dynamic_slice_in_dim(keys_new, first_row, T_DEV, 0)
        value_block = lax.dynamic_slice_in_dim(values_new, first_row, T_DEV, 0)
        query_heads = query_block.astype(jnp.float32).reshape(T_DEV, HEADS, HD)
        key_heads = key_block.astype(jnp.float32).reshape(T_DEV, HEADS, HD)
        value_heads = value_block.astype(jnp.float32).reshape(T_DEV, HEADS, HD)
        slot_index = (cache_owner[b] * SLOTS + cache_slot[b]).astype(jnp.int32)
        prior_keys = cache_keys[slot_index].astype(jnp.float32).reshape(SLOTS * PMAX, HEADS, HD)
        prior_values = cache_values[slot_index].astype(jnp.float32).reshape(SLOTS * PMAX, HEADS, HD)
        own_scores = jnp.einsum('thd,shd->hts', query_heads, key_heads) * score_scale
        own_live = (segment[:, None] == segment[None, :]) & (positions[None, :] <= positions[:, None])
        prior_scores = jnp.einsum('thd,shd->hts', query_heads, prior_keys) * score_scale
        prior_limit = prior_len[b][slot_of]
        prior_live = (segment[:, None] == slot_of[None, :]) & (row_in_slot < prior_limit)[None, :]
        live_mask = jnp.concatenate([own_live, prior_live], axis=1)
        scores = jnp.concatenate([own_scores, prior_scores], axis=2)
        scores = jnp.where(live_mask[None], scores, -1e+30)
        row_top = lax.optimization_barrier(jnp.max(scores, axis=2, keepdims=True))
        weights = jnp.where(live_mask[None], jnp.exp(scores - row_top), 0.0)
        row_total = lax.optimization_barrier(jnp.sum(weights, axis=2))
        rounded = lax.optimization_barrier(weights.astype(jnp.bfloat16)).astype(jnp.float32)
        all_values = jnp.concatenate([value_heads, prior_values], axis=0)
        numerator = jnp.einsum('hts,shd->thd', rounded, all_values)
        attended = (numerator / row_total.T[:, :, None]).reshape(T_DEV, ATT).astype(jnp.bfloat16)
        mixed = jnp.dot(attended, out_proj, preferred_element_type=jnp.float32).astype(jnp.bfloat16)
        padded_keys = jnp.pad(key_block, ((0, NEWCAP), (0, 0)))
        padded_values = jnp.pad(value_block, ((0, NEWCAP), (0, 0)))
        key_rows = []
        value_rows = []
        for j in range(SLOTS):
            keep = (row_marks < req_lens[j])[:, None]
            key_rows.append(jnp.where(keep, lax.dynamic_slice_in_dim(padded_keys, starts[j], NEWCAP, 0), jnp.zeros((), jnp.bfloat16)))
            value_rows.append(jnp.where(keep, lax.dynamic_slice_in_dim(padded_values, starts[j], NEWCAP, 0), jnp.zeros((), jnp.bfloat16)))
        return (mixed, jnp.stack(key_rows), jnp.stack(value_rows), slot_index)
    mixed, key_rows, value_rows, slot_index = lax.map(one_block, jnp.arange(N_REQ, dtype=jnp.int32))
    flat_index = slot_index.reshape(-1)
    new_keys = jnp.zeros((N_REQ * SLOTS, NEWCAP, ATT), jnp.bfloat16).at[flat_index].set(key_rows.reshape(N_REQ * SLOTS, NEWCAP, ATT))
    new_values = jnp.zeros((N_REQ * SLOTS, NEWCAP, ATT), jnp.bfloat16).at[flat_index].set(value_rows.reshape(N_REQ * SLOTS, NEWCAP, ATT))
    return (mixed.reshape(TOKENS, D), new_keys, new_values)
```

```python
import math

import jax
import jax.numpy as jnp
from jax import lax
from jax.experimental import pallas as pl
from jax.experimental.pallas import tpu as pltpu
from jax.sharding import PartitionSpec as P

HD = 224
NEWCAP = 192
LANES = 128
GROUP = 4
WIDTH = GROUP * HD
FLOOR = -1e30
SCALE = 1.0 / math.sqrt(HD)
VMEM_LIMIT = 48 * 1024 * 1024


def shifted(value, axis, steps):
    count = lax.axis_size(axis)
    pairs = [(source, (source + steps) % count) for source in range(count)]
    return lax.ppermute(value, axis, pairs)


def lane_iota(rows, columns):
    return lax.broadcasted_iota(jnp.int32, (rows, columns), 1)


def attend_heads(query, key, value, live):
    rows = query.shape[0]
    tiles = [None] * (WIDTH // LANES)
    logs = []
    for head in range(GROUP):
        low, high = head * HD, (head + 1) * HD
        first, last = low // LANES, -(-high // LANES)
        a, b = first * LANES, last * LANES
        columns = lane_iota(rows, b - a)
        inside = (columns >= low - a) & (columns < high - a)
        part = jnp.where(inside, query[:, a:b], jnp.zeros((), query.dtype))
        scores = lax.dot_general(
            part, key[:, a:b], (((1,), (1,)), ((), ())), preferred_element_type=jnp.float32
        )
        scores = jnp.where(live, scores * SCALE, FLOOR)
        top = jnp.max(scores, axis=1, keepdims=True)
        weights = jnp.exp(scores - top)
        total = jnp.sum(weights, axis=1, keepdims=True)
        out = jnp.dot(
            weights.astype(jnp.bfloat16), value[:, a:b], preferred_element_type=jnp.float32
        ) / total
        logs.append(top + jnp.log(total))
        for tile in range(first, last):
            piece = out[:, tile * LANES - a : (tile + 1) * LANES - a]
            if tile * LANES < low:
                piece = jnp.where(
                    lane_iota(rows, LANES) >= low - tile * LANES, piece, tiles[tile]
                )
            tiles[tile] = piece
    return tiles, logs


def own_kernel(starts_ref, query_ref, key_ref, value_ref, out_ref, log_ref):
    group = pl.program_id(0)
    rows = query_ref.shape[0]
    block = 256

    @pl.when(group == 0)
    def _():
        log_ref[...] = jnp.zeros_like(log_ref)

    for begin in range(0, rows, block):
        end = begin + block
        row = begin + lax.broadcasted_iota(jnp.int32, (block, end), 0)
        column = lane_iota(block, end)
        first = jnp.zeros((block, end), jnp.int32)
        for j in range(1, starts_ref.shape[0]):
            first = jnp.where(row >= starts_ref[j], starts_ref[j], first)
        live = (column >= first) & (column <= row)
        tiles, logs = attend_heads(
            query_ref[begin:end, :], key_ref[:end, :], value_ref[:end, :], live
        )
        for tile, piece in enumerate(tiles):
            out_ref[begin:end, tile * LANES : (tile + 1) * LANES] = piece.astype(out_ref.dtype)
        lanes = lane_iota(block, LANES)
        stat = log_ref[begin:end, :]
        for head in range(GROUP):
            stat = jnp.where(lanes == group * GROUP + head, logs[head], stat)
        log_ref[begin:end, :] = stat


def prior_kernel(info_ref, query_ref, key_ref, value_ref, out_ref):
    group = pl.program_id(0)
    rows = query_ref.shape[0]
    feat = out_ref.shape[1] - LANES

    @pl.when(group == 0)
    def _():
        out_ref[:, feat:] = jnp.zeros((rows, LANES), out_ref.dtype)

    live = lane_iota(rows, key_ref.shape[1]) < info_ref[1]
    tiles, logs = attend_heads(query_ref[...], key_ref[0], value_ref[0], live)
    for tile, piece in enumerate(tiles):
        place = pl.ds(pl.multiple_of(group * WIDTH + tile * LANES, LANES), LANES)
        out_ref[:, place] = piece.astype(out_ref.dtype)
    lanes = lane_iota(rows, LANES)
    stat = out_ref[:, feat:].astype(jnp.float32)
    for head in range(GROUP):
        rest = logs[head]
        for part in range(3):
            rounded = rest.astype(jnp.bfloat16).astype(jnp.float32)
            stat = jnp.where(lanes == (group * GROUP + head) * 3 + part, rounded, stat)
            rest = rest - rounded
    out_ref[:, feat:] = stat.astype(out_ref.dtype)


def project_kernel(info_ref, own_ref, log_ref, plus_ref, minus_ref, weight_ref, out_ref, held):
    rows, feat = own_ref.shape
    cap = plus_ref.shape[0]

    @pl.when(pl.program_id(0) == 0)
    def _():
        spread = []
        row = lax.broadcasted_iota(jnp.int32, (rows, cap), 0)
        column = lane_iota(rows, cap)
        for d in range(2):
            start, count = info_ref[2 * d], info_ref[2 * d + 1]
            hit = (row - start == column) & (column < count)
            spread.append(jnp.where(hit, 1.0, 0.0).astype(jnp.bfloat16))

        def placed(a, b):
            return jnp.dot(
                spread[0], plus_ref[:, a:b], preferred_element_type=jnp.float32
            ) + jnp.dot(spread[1], minus_ref[:, a:b], preferred_element_type=jnp.float32)

        stat = placed(feat, feat + LANES)
        mine = log_ref[...]
        marks = lax.broadcasted_iota(jnp.int32, (rows, 1), 0)
        has = marks < info_ref[1] + info_ref[3]
        own_part, prior_part = [], []
        for head in range(feat // HD):
            far = stat[:, 3 * head : 3 * head + 1]
            far = far + stat[:, 3 * head + 1 : 3 * head + 2]
            far = far + stat[:, 3 * head + 2 : 3 * head + 3]
            near = mine[:, head : head + 1]
            top = jnp.maximum(near, far)
            x, y = jnp.exp(near - top), jnp.exp(far - top)
            own_part.append(jnp.where(has, x / (x + y), 1.0))
            prior_part.append(jnp.where(has, y / (x + y), 0.0))
        lanes = lane_iota(rows, LANES)
        for tile in range(feat // LANES):
            a, b = tile * LANES, (tile + 1) * LANES
            h0, h1 = a // HD, (b - 1) // HD
            x, y = own_part[h0], prior_part[h0]
            if h1 != h0:
                x = jnp.where(lanes < h1 * HD - a, x, own_part[h1])
                y = jnp.where(lanes < h1 * HD - a, y, prior_part[h1])
            both = own_ref[:, a:b].astype(jnp.float32) * x + placed(a, b) * y
            held[:, a:b] = both.astype(jnp.bfloat16)

    out_ref[...] = jnp.dot(
        held[...], weight_ref[...], preferred_element_type=jnp.float32
    ).astype(out_ref.dtype)


def own_attention(starts, queries, keys, values):
    rows, feat = queries.shape
    spec = pl.BlockSpec((rows, WIDTH), lambda g, s: (0, g))
    return pl.pallas_call(
        own_kernel,
        grid_spec=pltpu.PrefetchScalarGridSpec(
            num_scalar_prefetch=1,
            grid=(feat // WIDTH,),
            in_specs=[spec] * 3,
            out_specs=[spec, pl.BlockSpec((rows, LANES), lambda g, s: (0, 0))],
        ),
        out_shape=[
            jax.ShapeDtypeStruct((rows, feat), jnp.bfloat16),
            jax.ShapeDtypeStruct((rows, LANES), jnp.float32),
        ],
        compiler_params=pltpu.CompilerParams(vmem_limit_bytes=VMEM_LIMIT),
        cost_estimate=pl.CostEstimate(
            flops=20_000_000_000, bytes_accessed=9_000_000, transcendentals=2_000_000
        ),
        name="own_attention",
    )(starts, queries, keys, values)


def prior_attention(info, queries, cache_keys, cache_values):
    rows, feat = queries.shape
    prior = cache_keys.shape[1]
    cache = pl.BlockSpec((1, prior, WIDTH), lambda g, s: (s[0], 0, g))
    return pl.pallas_call(
        prior_kernel,
        grid_spec=pltpu.PrefetchScalarGridSpec(
            num_scalar_prefetch=1,
            grid=(feat // WIDTH,),
            in_specs=[pl.BlockSpec((rows, WIDTH), lambda g, s: (0, g)), cache, cache],
            out_specs=pl.BlockSpec((rows, feat + LANES), lambda g, s: (0, 0)),
        ),
        out_shape=jax.ShapeDtypeStruct((rows, feat + LANES), jnp.bfloat16),
        compiler_params=pltpu.CompilerParams(vmem_limit_bytes=VMEM_LIMIT),
        cost_estimate=pl.CostEstimate(
            flops=10_000_000_000, bytes_accessed=9_000_000, transcendentals=2_000_000
        ),
        name="prior_attention",
    )(info, queries, cache_keys, cache_values)


def project(info, own, logs, plus, minus, weight):
    rows, feat = own.shape
    columns = weight.shape[1]
    block = 512

    def whole(array):
        return pl.BlockSpec(array.shape, lambda n, s: (0, 0))

    return pl.pallas_call(
        project_kernel,
        grid_spec=pltpu.PrefetchScalarGridSpec(
            num_scalar_prefetch=1,
            grid=(columns // block,),
            in_specs=[
                whole(own),
                whole(logs),
                whole(plus),
                whole(minus),
                pl.BlockSpec((feat, block), lambda n, s: (0, n)),
            ],
            out_specs=pl.BlockSpec((rows, block), lambda n, s: (0, n)),
            scratch_shapes=[pltpu.VMEM((rows, feat), jnp.bfloat16)],
        ),
        out_shape=jax.ShapeDtypeStruct((rows, columns), jnp.bfloat16),
        compiler_params=pltpu.CompilerParams(vmem_limit_bytes=VMEM_LIMIT),
        cost_estimate=pl.CostEstimate(
            flops=2 * rows * feat * columns, bytes_accessed=22_000_000, transcendentals=0
        ),
        name="project",
    )(info, own, logs, plus, minus, weight)


def pick_rows(source, start, count):
    row = lax.broadcasted_iota(jnp.int32, (NEWCAP, source.shape[0]), 0)
    column = lane_iota(NEWCAP, source.shape[0])
    hit = (column - start == row) & (row < count)
    return jnp.dot(
        hit.astype(jnp.bfloat16), source, preferred_element_type=jnp.float32
    ).astype(jnp.bfloat16)


def body(
    queries,
    keys_new,
    values_new,
    cache_keys,
    cache_values,
    out_proj,
    req_lengths,
    cache_owner,
    cache_slot,
    prior_len,
):
    slot_count = cache_keys.shape[0]
    lens = [req_lengths[0, j] for j in range(req_lengths.shape[1])]
    starts = [jnp.int32(0)]
    for j in range(1, len(lens)):
        starts.append(starts[-1] + lens[j - 1])
    count = lax.axis_size("req")
    me = lax.axis_index("req")
    next_is_first = cache_owner[0, 0] == lax.rem(me + 1, count)

    def by_way(a, b):
        return jnp.where(next_is_first, a, b), jnp.where(next_is_first, b, a)

    start = by_way(starts[0], starts[1])
    length = by_way(lens[0], lens[1])
    slot = by_way(cache_slot[0, 0], cache_slot[0, 1])
    prior = by_way(prior_len[0, 0], prior_len[0, 1])
    ways = (1, -1)

    tags = [shifted(jnp.stack([slot[d], prior[d]]), "req", ways[d]) for d in range(2)]
    asked = [shifted(pick_rows(queries, start[d], length[d]), "req", ways[d]) for d in range(2)]
    own, logs = own_attention(jnp.stack(starts), queries, keys_new, values_new)
    sent_keys = [pick_rows(keys_new, start[d], length[d]) for d in range(2)]
    sent_values = [pick_rows(values_new, start[d], length[d]) for d in range(2)]

    sent_keys, asked = lax.optimization_barrier((sent_keys, asked))
    got_keys = [shifted(sent_keys[d], "req", ways[d]) for d in range(2)]
    answers = [prior_attention(tags[d], asked[d], cache_keys, cache_values) for d in range(2)]
    back = [shifted(answers[d], "req", -ways[d]) for d in range(2)]
    sent_values, back = lax.optimization_barrier((sent_values, back))
    got_values = [shifted(sent_values[d], "req", ways[d]) for d in range(2)]

    info = jnp.stack([start[0], length[0], start[1], length[1]])
    mixed = project(info, own, logs, back[0], back[1], out_proj)
    mixed = lax.psum_scatter(mixed, "tp", scatter_dimension=0, tiled=True)

    slot_ids = jnp.arange(slot_count, dtype=jnp.int32)[:, None, None]
    new_keys = jnp.where(slot_ids == tags[0][0], got_keys[0][None], got_keys[1][None])
    new_values = jnp.where(slot_ids == tags[0][0], got_values[0][None], got_values[1][None])
    return (mixed, new_keys, new_values)


def solution(mesh):
    in_specs = (
        P("req", "tp"),
        P("req", "tp"),
        P("req", "tp"),
        P("req", None, "tp"),
        P("req", None, "tp"),
        P("tp", None),
        P("req", None),
        P("req", None),
        P("req", None),
        P("req", None),
    )
    out_specs = (P(("req", "tp"), None), P("req", None, "tp"), P("req", None, "tp"))
    return jax.shard_map(body, mesh=mesh, in_specs=in_specs, out_specs=out_specs, check_vma=False)
```

```python
import functools
import math

import jax
import jax.numpy as jnp
from jax import lax
from jax.experimental import pallas as pl
from jax.experimental.pallas import tpu as pltpu
from jax.sharding import PartitionSpec as P

HD = 224
NEWCAP = 192
LANES = 128
GROUP = 4
WIDTH = GROUP * HD
FLOOR = -1e30
SCALE = 1.0 / math.sqrt(HD)
VMEM_LIMIT = 60 * 1024 * 1024
MESH = pl.DeviceIdType.MESH
WAYS = (1, -1)


def lane_iota(rows, columns):
    return lax.broadcasted_iota(jnp.int32, (rows, columns), 1)


def row_iota(rows, columns):
    return lax.broadcasted_iota(jnp.int32, (rows, columns), 0)


def attend_heads(query_of, key_of, value_of, live):
    tiles = [None] * (WIDTH // LANES)
    logs = []
    for head in range(GROUP):
        low, high = head * HD, (head + 1) * HD
        first, last = low // LANES, -(-high // LANES)
        a, b = first * LANES, last * LANES
        query = query_of(a, b)
        rows = query.shape[0]
        columns = lane_iota(rows, b - a)
        inside = (columns >= low - a) & (columns < high - a)
        part = jnp.where(inside, query, jnp.zeros((), query.dtype))
        scores = lax.dot_general(
            part, key_of(a, b), (((1,), (1,)), ((), ())), preferred_element_type=jnp.float32
        )
        scores = jnp.where(live, scores * SCALE, FLOOR)
        top = jnp.max(scores, axis=1, keepdims=True)
        weights = jnp.exp(scores - top)
        total = jnp.sum(weights, axis=1, keepdims=True)
        out = jnp.dot(
            weights.astype(jnp.bfloat16), value_of(a, b), preferred_element_type=jnp.float32
        ) / total
        logs.append(top + jnp.log(total))
        for tile in range(first, last):
            piece = out[:, tile * LANES - a : (tile + 1) * LANES - a]
            if tile * LANES < low:
                piece = jnp.where(
                    lane_iota(rows, LANES) >= low - tile * LANES, piece, tiles[tile]
                )
            tiles[tile] = piece
    return tiles, logs


def place(group, a, b):
    return pl.ds(pl.multiple_of(group * WIDTH + a, LANES), b - a)


def whole_kernel(
    count, chips, lens_ref, owner_ref, slot_ref, prior_ref,
    query_hbm, key_hbm, value_hbm, cache_key_hbm, cache_value_hbm, weight_hbm,
    mixed_ref, got_keys, got_values, tag_out,
    query, key, value, cache_key, cache_value, weight,
    query_out, key_out, value_out, query_in, tag_send, tag_in,
    result, answer, back, own, logs, held, part_a, part_b,
    near_a, near_b, far_send, far_in, local_sem, send_sem, recv_sem,
):
    rows, feat = query.shape
    cap = query_out.shape[1]
    prior = cache_key.shape[1]
    half = rows // 2
    span = rows // chips
    chunk = span // 2
    me, tp = lax.axis_index("req"), lax.axis_index("tp")
    chip, core = lax.div(tp, 2), lax.rem(tp, 2)
    sibling = chip * 2 + (1 - core)
    others = [lax.rem(chip + o, chips) for o in range(1, chips)]
    across = [other * 2 + core for other in others]
    beside = [lax.rem(me + 1, count), lax.rem(me + count - 1, count)]

    locals_ = [
        pltpu.make_async_copy(source, target, local_sem.at[i])
        for i, (source, target) in enumerate(
            (
                (query_hbm, query),
                (key_hbm, key),
                (value_hbm, value),
                (cache_key_hbm, cache_key),
                (cache_value_hbm, cache_value),
                (weight_hbm, weight),
            )
        )
    ]
    for copy in locals_:
        copy.start()

    barrier = pltpu.get_barrier_semaphore()
    partners = [{"req": beside[0]}, {"req": beside[1]}, {"tp": sibling}]
    partners += [{"tp": other} for other in across]
    for target in partners:
        pl.semaphore_signal(barrier, inc=1, device_id=target, device_id_type=MESH)
    pl.semaphore_wait(barrier, len(partners))

    def remote(number, source, target, device):
        return pltpu.make_async_remote_copy(
            src_ref=source,
            dst_ref=target,
            send_sem=send_sem.at[number],
            recv_sem=recv_sem.at[number],
            device_id=device,
            device_id_type=MESH,
        )

    def to_side(number, source, target, d, forth=True):
        device = {"req": beside[d] if forth else beside[1 - d]}
        return remote(number + d, source.at[d], target.at[d], device)

    starts = [jnp.int32(0)]
    for j in range(1, lens_ref.shape[1]):
        starts.append(starts[-1] + lens_ref[0, j - 1])
    next_is_first = owner_ref[0, 0] == beside[0]

    def by_way(a, b):
        return [jnp.where(next_is_first, a, b), jnp.where(next_is_first, b, a)]

    start = by_way(starts[0], starts[1])
    length = by_way(lens_ref[0, 0], lens_ref[0, 1])
    slot = by_way(slot_ref[0, 0], slot_ref[0, 1])
    limit = by_way(prior_ref[0, 0], prior_ref[0, 1])

    def pack(source, target, d):
        row, column = row_iota(cap, rows), lane_iota(cap, rows)
        hit = (column - start[d] == row) & (row < length[d])
        pick = jnp.where(hit, 1.0, 0.0).astype(jnp.bfloat16)

        def step(n, carry):
            at = pl.ds(pl.multiple_of(n * 256, 256), 256)
            target[d, :, at] = jnp.dot(
                pick, source[:, at], preferred_element_type=jnp.float32
            ).astype(jnp.bfloat16)
            return carry

        lax.fori_loop(0, feat // 256, step, 0)

    locals_[0].wait()
    tags, asks = [], []
    for d in range(2):
        tag_send[d] = jnp.where(row_iota(8, prior) == 0, slot[d], limit[d])
        pack(query, query_out, d)
        tags.append(to_side(0, tag_send, tag_in, d))
        asks.append(to_side(2, query_out, query_in, d))
        tags[d].start()
        asks[d].start()

    locals_[1].wait()
    locals_[2].wait()
    for d in range(2):
        pack(key, key_out, d)
        pack(value, value_out, d)

    logs[...] = jnp.zeros_like(logs)

    def own_group(group, carry):
        for begin in range(0, rows, half):
            end = begin + half
            row, column = begin + row_iota(half, end), lane_iota(half, end)
            first = jnp.zeros((half, end), jnp.int32)
            for s in starts[1:]:
                first = jnp.where(row >= s, s, first)
            tiles, sums = attend_heads(
                lambda a, b: query[begin:end, place(group, a, b)],
                lambda a, b: key[:end, place(group, a, b)],
                lambda a, b: value[:end, place(group, a, b)],
                (column >= first) & (column <= row),
            )
            for tile, piece in enumerate(tiles):
                at = place(group, tile * LANES, (tile + 1) * LANES)
                own[begin:end, at] = piece.astype(own.dtype)
            lanes = lane_iota(half, LANES)
            stat = logs[begin:end, :]
            for head in range(GROUP):
                stat = jnp.where(lanes == group * GROUP + head, sums[head], stat)
            logs[begin:end, :] = stat
        return carry

    lax.fori_loop(0, feat // WIDTH, own_group, 0)

    for d in range(2):
        tags[d].wait()
        asks[d].wait()
    key_sends = [to_side(4, key_out, got_keys, d) for d in range(2)]
    for copy in key_sends:
        copy.start()
    locals_[3].wait()
    locals_[4].wait()

    for i in range(2):
        result[i, :, feat:] = jnp.zeros((cap, LANES), result.dtype)

    groups = feat // WIDTH

    def prior_group(n, carry):
        i, group = n // groups, n % groups
        from_first = tag_in[0, 0:1, :] == i
        reach = jnp.where(from_first, tag_in[0, 1:2, :], tag_in[1, 1:2, :])

        def asked(a, b):
            at = place(group, a, b)
            first = jnp.broadcast_to(
                jnp.where(from_first[:, : b - a], 1.0, 0.0), (cap, b - a)
            )
            return jnp.where(
                first > 0.5,
                query_in[0, :, at].astype(jnp.float32),
                query_in[1, :, at].astype(jnp.float32),
            ).astype(jnp.bfloat16)

        tiles, sums = attend_heads(
            asked,
            lambda a, b: cache_key[i, :, place(group, a, b)],
            lambda a, b: cache_value[i, :, place(group, a, b)],
            lane_iota(cap, prior) < reach,
        )
        for tile, piece in enumerate(tiles):
            at = place(group, tile * LANES, (tile + 1) * LANES)
            result[i, :, at] = piece.astype(result.dtype)
        lanes = lane_iota(cap, LANES)
        stat = result[i, :, feat:].astype(jnp.float32)
        for head in range(GROUP):
            rest = sums[head]
            for part in range(3):
                rounded = rest.astype(jnp.bfloat16).astype(jnp.float32)
                stat = jnp.where(lanes == (group * GROUP + head) * 3 + part, rounded, stat)
                rest = rest - rounded
        result[i, :, feat:] = stat.astype(result.dtype)
        return carry

    lax.fori_loop(0, 2 * groups, prior_group, 0)

    def choose(n, carry):
        at = pl.ds(pl.multiple_of(n * LANES, LANES), LANES)
        first = jnp.broadcast_to(
            jnp.where(tag_in[0, 0:1, :LANES] == 0, 1.0, 0.0), (cap, LANES)
        )
        x, y = result[0, :, at].astype(jnp.float32), result[1, :, at].astype(jnp.float32)
        answer[0, :, at] = jnp.where(first > 0.5, x, y).astype(answer.dtype)
        answer[1, :, at] = jnp.where(first > 0.5, y, x).astype(answer.dtype)
        return carry

    lax.fori_loop(0, (feat + LANES) // LANES, choose, 0)
    tag_out[...] = tag_in[0, :, :LANES]
    backs = [to_side(6, answer, back, d, forth=False) for d in range(2)]
    for copy in backs:
        copy.start()
    for copy in backs:
        copy.wait()
    value_sends = [to_side(8, value_out, got_values, d) for d in range(2)]
    for copy in value_sends:
        copy.start()

    def merge(base):
        at_rows = pl.ds(pl.multiple_of(base, span), span)
        row, column = base + row_iota(span, cap), lane_iota(span, cap)
        spread = []
        for d in range(2):
            hit = (row - start[d] == column) & (column < length[d])
            spread.append(jnp.where(hit, 1.0, 0.0).astype(jnp.bfloat16))

        def placed(a, b):
            return jnp.dot(
                spread[0], back[0, :, a:b], preferred_element_type=jnp.float32
            ) + jnp.dot(spread[1], back[1, :, a:b], preferred_element_type=jnp.float32)

        stat = placed(feat, feat + LANES)
        mine = logs[at_rows, :]
        has = base + row_iota(span, 1) < starts[2]
        own_part, prior_part = [], []
        for head in range(feat // HD):
            far = stat[:, 3 * head : 3 * head + 1]
            far = far + stat[:, 3 * head + 1 : 3 * head + 2]
            far = far + stat[:, 3 * head + 2 : 3 * head + 3]
            near = mine[:, head : head + 1]
            top = jnp.maximum(near, far)
            x, y = jnp.exp(near - top), jnp.exp(far - top)
            own_part.append(jnp.where(has, x / (x + y), 1.0))
            prior_part.append(jnp.where(has, y / (x + y), 0.0))
        lanes = lane_iota(span, LANES)
        for pair in range(feat // 256):
            both = placed(pair * 256, pair * 256 + 256)
            for side in range(2):
                a = pair * 256 + side * LANES
                b = a + LANES
                h0, h1 = a // HD, (b - 1) // HD
                x, y = own_part[h0], prior_part[h0]
                if h1 != h0:
                    x = jnp.where(lanes < h1 * HD - a, x, own_part[h1])
                    y = jnp.where(lanes < h1 * HD - a, y, prior_part[h1])
                far = both[:, side * LANES : side * LANES + LANES]
                total = own[at_rows, a:b].astype(jnp.float32) * x + far * y
                held[:, a:b] = total.astype(jnp.bfloat16)

    def project(target):
        def step(n, carry):
            at = pl.ds(pl.multiple_of(n * 512, 512), 512)
            target[:, at] = jnp.dot(
                held[...], weight[:, at], preferred_element_type=jnp.float32
            ).astype(target.dtype)
            return carry

        lax.fori_loop(0, weight.shape[1] // 512, step, 0)

    def chunk_of(n):
        return pl.ds(pl.multiple_of(n * chunk, chunk), chunk)

    locals_[5].wait()
    overs = []
    for n in range(chips - 1):
        merge(others[n] * span)
        project(part_a.at[n])
        near = remote(
            11 + n, part_a.at[n, chunk_of(1 - core), :], near_a.at[n], {"tp": sibling}
        )
        near.start()
        near.wait()
        far_send[n] = (
            part_a[n, chunk_of(core), :].astype(jnp.float32) + near_a[n].astype(jnp.float32)
        ).astype(far_send.dtype)
        overs.append(
            remote(10 + chips + n, far_send.at[n], far_in.at[n], {"tp": across[n]})
        )
        overs[n].start()
    merge(chip * span)
    project(part_b)
    last = remote(10, part_b.at[chunk_of(1 - core), :], near_b, {"tp": sibling})
    last.start()
    last.wait()
    total = part_b[chunk_of(core), :].astype(jnp.float32) + near_b[...].astype(jnp.float32)
    for n in range(chips - 1):
        overs[n].wait()
        total = total + far_in[n].astype(jnp.float32)
    mixed_ref[...] = total.astype(mixed_ref.dtype)
    for copy in key_sends + value_sends:
        copy.wait()


def body(
    queries,
    keys_new,
    values_new,
    cache_keys,
    cache_values,
    out_proj,
    req_lengths,
    cache_owner,
    cache_slot,
    prior_len,
):
    rows, feat = queries.shape
    width = out_proj.shape[1]
    slots, prior = cache_keys.shape[:2]
    chips = lax.axis_size("tp") // 2
    span = rows // chips
    chunk = span // 2
    bf16 = jnp.bfloat16
    packed = (2, NEWCAP, feat)
    answers = (2, NEWCAP, feat + LANES)
    smem = pl.BlockSpec(memory_space=pltpu.SMEM)
    hbm = pl.BlockSpec(memory_space=pl.ANY)
    vmem = pl.BlockSpec(memory_space=pltpu.VMEM)
    mixed, got_keys, got_values, tag = pl.pallas_call(
        functools.partial(whole_kernel, lax.axis_size("req"), chips),
        in_specs=[smem] * 4 + [hbm] * 6,
        out_specs=[vmem, hbm, hbm, vmem],
        out_shape=[
            jax.ShapeDtypeStruct((chunk, width), bf16),
            jax.ShapeDtypeStruct(packed, bf16),
            jax.ShapeDtypeStruct(packed, bf16),
            jax.ShapeDtypeStruct((8, LANES), jnp.int32),
        ],
        scratch_shapes=[
            pltpu.VMEM((rows, feat), bf16),
            pltpu.VMEM((rows, feat), bf16),
            pltpu.VMEM((rows, feat), bf16),
            pltpu.VMEM(cache_keys.shape, bf16),
            pltpu.VMEM(cache_values.shape, bf16),
            pltpu.VMEM(out_proj.shape, bf16),
            pltpu.VMEM(packed, bf16),
            pltpu.VMEM(packed, bf16),
            pltpu.VMEM(packed, bf16),
            pltpu.VMEM(packed, bf16),
            pltpu.VMEM((2, 8, prior), jnp.int32),
            pltpu.VMEM((2, 8, prior), jnp.int32),
            pltpu.VMEM(answers, bf16),
            pltpu.VMEM(answers, bf16),
            pltpu.VMEM(answers, bf16),
            pltpu.VMEM((rows, feat), bf16),
            pltpu.VMEM((rows, LANES), jnp.float32),
            pltpu.VMEM((span, feat), bf16),
            pltpu.VMEM((chips - 1, span, width), bf16),
            pltpu.VMEM((span, width), bf16),
            pltpu.VMEM((chips - 1, chunk, width), bf16),
            pltpu.VMEM((chunk, width), bf16),
            pltpu.VMEM((chips - 1, chunk, width), bf16),
            pltpu.VMEM((chips - 1, chunk, width), bf16),
            pltpu.SemaphoreType.DMA((6,)),
            pltpu.SemaphoreType.DMA((9 + 2 * chips,)),
            pltpu.SemaphoreType.DMA((9 + 2 * chips,)),
        ],
        compiler_params=pltpu.CompilerParams(
            collective_id=0, has_side_effects=True, vmem_limit_bytes=VMEM_LIMIT
        ),
        cost_estimate=pl.CostEstimate(
            flops=2 * rows * feat * width, bytes_accessed=37_000_000, transcendentals=5_000_000
        ),
        name="whole",
    )(
        req_lengths, cache_owner, cache_slot, prior_len,
        queries, keys_new, values_new, cache_keys, cache_values, out_proj,
    )
    slot_ids = jnp.arange(slots, dtype=jnp.int32)[:, None, None]
    first = slot_ids == tag[0, 0]
    new_keys = jnp.where(first, got_keys[0][None], got_keys[1][None])
    new_values = jnp.where(first, got_values[0][None], got_values[1][None])
    return (mixed, new_keys, new_values)


def solution(mesh):
    in_specs = (
        P("req", "tp"),
        P("req", "tp"),
        P("req", "tp"),
        P("req", None, "tp"),
        P("req", None, "tp"),
        P("tp", None),
        P("req", None),
        P("req", None),
        P("req", None),
        P("req", None),
    )
    out_specs = (P(("req", "tp"), None), P("req", None, "tp"), P("req", None, "tp"))
    return jax.shard_map(body, mesh=mesh, in_specs=in_specs, out_specs=out_specs, check_vma=False)
```

```python
import functools
import math

import jax
import jax.numpy as jnp
from jax import lax
from jax.experimental import pallas as pl
from jax.experimental.pallas import tpu as pltpu
from jax.sharding import PartitionSpec as P

HD = 224
NEWCAP = 192
LANES = 128
GROUP = 4
WIDTH = GROUP * HD
FLOOR = -1e30
SCALE = 1.0 / math.sqrt(HD)
VMEM_LIMIT = 60 * 1024 * 1024
MESH = pl.DeviceIdType.MESH
WAYS = (1, -1)


def lane_iota(rows, columns):
    return lax.broadcasted_iota(jnp.int32, (rows, columns), 1)


def row_iota(rows, columns):
    return lax.broadcasted_iota(jnp.int32, (rows, columns), 0)


def attend_heads(query_of, key_of, value_of, live):
    tiles = [None] * (WIDTH // LANES)
    logs = []
    for head in range(GROUP):
        low, high = head * HD, (head + 1) * HD
        first, last = low // LANES, -(-high // LANES)
        a, b = first * LANES, last * LANES
        query = query_of(a, b)
        rows = query.shape[0]
        columns = lane_iota(rows, b - a)
        inside = (columns >= low - a) & (columns < high - a)
        part = jnp.where(inside, query, jnp.zeros((), query.dtype))
        scores = lax.dot_general(
            part, key_of(a, b), (((1,), (1,)), ((), ())), preferred_element_type=jnp.float32
        )
        scores = jnp.where(live, scores * SCALE, FLOOR)
        top = jnp.max(scores, axis=1, keepdims=True)
        weights = jnp.exp(scores - top)
        total = jnp.sum(weights, axis=1, keepdims=True)
        out = jnp.dot(
            weights.astype(jnp.bfloat16), value_of(a, b), preferred_element_type=jnp.float32
        ) / total
        logs.append(top + jnp.log(total))
        for tile in range(first, last):
            piece = out[:, tile * LANES - a : (tile + 1) * LANES - a]
            if tile * LANES < low:
                piece = jnp.where(
                    lane_iota(rows, LANES) >= low - tile * LANES, piece, tiles[tile]
                )
            tiles[tile] = piece
    return tiles, logs


def place(group, a, b):
    return pl.ds(pl.multiple_of(group * WIDTH + a, LANES), b - a)


def whole_kernel(
    count, chips, lens_ref, owner_ref, slot_ref, prior_ref,
    query_hbm, key_hbm, value_hbm, cache_key_hbm, cache_value_hbm, weight_hbm,
    mixed_ref, got_key_first, got_key_second, got_value_first, got_value_second, tag_out,
    query, key, value, cache_key, cache_value, weight,
    query_out, key_out, value_out, query_in, tag_send, tag_in,
    result, sums_out, answer, back, sums_answer, sums_back, own, logs, held, part_a, part_b,
    near_a, near_b, far_send, far_in, local_sem, send_sem, recv_sem,
):
    rows, feat = query.shape
    cap = query_out.shape[1]
    prior = cache_key.shape[1]
    half = rows // 2
    span = rows // chips
    chunk = span // 2
    me, tp = lax.axis_index("req"), lax.axis_index("tp")
    chip, core = lax.div(tp, 2), lax.rem(tp, 2)
    sibling = chip * 2 + (1 - core)
    others = [lax.rem(chip + o, chips) for o in range(1, chips)]
    across = [other * 2 + core for other in others]
    beside = [lax.rem(me + 1, count), lax.rem(me + count - 1, count)]

    locals_ = [
        pltpu.make_async_copy(source, target, local_sem.at[i])
        for i, (source, target) in enumerate(
            (
                (query_hbm, query),
                (key_hbm, key),
                (value_hbm, value),
                (cache_key_hbm, cache_key),
                (cache_value_hbm, cache_value),
                (weight_hbm, weight),
            )
        )
    ]
    locals_[0].start()

    barrier = pltpu.get_barrier_semaphore()
    partners = [{"req": beside[0]}, {"req": beside[1]}, {"tp": sibling}]
    partners += [{"tp": other} for other in across]
    for target in partners:
        pl.semaphore_signal(barrier, inc=1, device_id=target, device_id_type=MESH)
    pl.semaphore_wait(barrier, len(partners))

    def remote(number, source, target, device):
        return pltpu.make_async_remote_copy(
            src_ref=source,
            dst_ref=target,
            send_sem=send_sem.at[number],
            recv_sem=recv_sem.at[number],
            device_id=device,
            device_id_type=MESH,
        )

    def to_side(number, source, target, d, forth=True):
        device = {"req": beside[d] if forth else beside[1 - d]}
        return remote(number + d, source.at[d], target.at[d], device)

    got_keys = (got_key_first, got_key_second)
    got_values = (got_value_first, got_value_second)

    def store_to(number, source, target, d, at):
        return remote(number + d, source.at[d, at, :], target[d].at[at, :], {"req": beside[d]})

    starts = [jnp.int32(0)]
    for j in range(1, lens_ref.shape[1]):
        starts.append(starts[-1] + lens_ref[0, j - 1])
    next_is_first = owner_ref[0, 0] == beside[0]

    def by_way(a, b):
        return [jnp.where(next_is_first, a, b), jnp.where(next_is_first, b, a)]

    start = by_way(starts[0], starts[1])
    length = by_way(lens_ref[0, 0], lens_ref[0, 1])
    slot = by_way(slot_ref[0, 0], slot_ref[0, 1])
    limit = by_way(prior_ref[0, 0], prior_ref[0, 1])

    def pack(source, target, d):
        row, column = row_iota(cap, rows), lane_iota(cap, rows)
        hit = (column - start[d] == row) & (row < length[d])
        pick = jnp.where(hit, 1.0, 0.0).astype(jnp.bfloat16)

        def step(n, carry):
            at = pl.ds(pl.multiple_of(n * 256, 256), 256)
            target[d, :, at] = jnp.dot(
                pick, source[:, at], preferred_element_type=jnp.float32
            ).astype(jnp.bfloat16)
            return carry

        lax.fori_loop(0, feat // 256, step, 0)

    locals_[0].wait()
    for copy in locals_[1:]:
        copy.start()
    tags, asks = [], []
    for d in range(2):
        tag_send[d] = jnp.where(row_iota(8, prior) == 0, slot[d], limit[d])
        pack(query, query_out, d)
        tags.append(to_side(0, tag_send, tag_in, d))
        asks.append(to_side(2, query_out, query_in, d))
        tags[d].start()
        asks[d].start()

    locals_[1].wait()
    locals_[2].wait()
    for d in range(2):
        pack(key, key_out, d)
        pack(value, value_out, d)

    logs[...] = jnp.zeros_like(logs)

    def own_group(group, carry):
        for begin in range(0, rows, half):
            end = begin + half
            row, column = begin + row_iota(half, end), lane_iota(half, end)
            first = jnp.zeros((half, end), jnp.int32)
            for s in starts[1:]:
                first = jnp.where(row >= s, s, first)
            tiles, sums = attend_heads(
                lambda a, b: query[begin:end, place(group, a, b)],
                lambda a, b: key[:end, place(group, a, b)],
                lambda a, b: value[:end, place(group, a, b)],
                (column >= first) & (column <= row),
            )
            for tile, piece in enumerate(tiles):
                at = place(group, tile * LANES, (tile + 1) * LANES)
                own[begin:end, at] = piece.astype(own.dtype)
            lanes = lane_iota(half, LANES)
            stat = logs[begin:end, :]
            for head in range(GROUP):
                stat = jnp.where(lanes == group * GROUP + head, sums[head], stat)
            logs[begin:end, :] = stat
        return carry

    lax.fori_loop(0, feat // WIDTH, own_group, 0)

    early, late = pl.ds(0, cap // 2), pl.ds(cap // 2, cap // 2)
    for d in range(2):
        tags[d].wait_send()
        asks[d].wait_send()
    stores = [store_to(4, key_out, got_keys, d, early) for d in range(2)]
    for copy in stores:
        copy.start()
    for d in range(2):
        tags[d].wait_recv()
        asks[d].wait_recv()
    locals_[3].wait()
    locals_[4].wait()

    for i in range(2):
        sums_out[i] = jnp.zeros((cap, LANES), sums_out.dtype)

    groups = feat // WIDTH

    def prior_group(n, carry):
        i, group = n // groups, n % groups
        from_first = tag_in[0, 0:1, :] == i
        reach = jnp.where(from_first, tag_in[0, 1:2, :], tag_in[1, 1:2, :])

        def asked(a, b):
            at = place(group, a, b)
            first = jnp.broadcast_to(
                jnp.where(from_first[:, : b - a], 1.0, 0.0), (cap, b - a)
            )
            return jnp.where(
                first > 0.5,
                query_in[0, :, at].astype(jnp.float32),
                query_in[1, :, at].astype(jnp.float32),
            ).astype(jnp.bfloat16)

        tiles, sums = attend_heads(
            asked,
            lambda a, b: cache_key[i, :, place(group, a, b)],
            lambda a, b: cache_value[i, :, place(group, a, b)],
            lane_iota(cap, prior) < reach,
        )
        for tile, piece in enumerate(tiles):
            at = place(group, tile * LANES, (tile + 1) * LANES)
            result[i, :, at] = piece.astype(result.dtype)
        lanes = lane_iota(cap, LANES)
        stat = sums_out[i].astype(jnp.float32)
        for head in range(GROUP):
            rest = sums[head]
            for part in range(3):
                rounded = rest.astype(jnp.bfloat16).astype(jnp.float32)
                stat = jnp.where(lanes == (group * GROUP + head) * 3 + part, rounded, stat)
                rest = rest - rounded
        sums_out[i] = stat.astype(sums_out.dtype)
        return carry

    lax.fori_loop(0, 2 * groups, prior_group, 0)

    def choose(n, carry):
        at = pl.ds(pl.multiple_of(n * LANES, LANES), LANES)
        first = jnp.broadcast_to(
            jnp.where(tag_in[0, 0:1, :LANES] == 0, 1.0, 0.0), (cap, LANES)
        )
        x, y = result[0, :, at].astype(jnp.float32), result[1, :, at].astype(jnp.float32)
        answer[0, :, at] = jnp.where(first > 0.5, x, y).astype(answer.dtype)
        answer[1, :, at] = jnp.where(first > 0.5, y, x).astype(answer.dtype)
        return carry

    lax.fori_loop(0, feat // LANES, choose, 0)
    first = jnp.broadcast_to(jnp.where(tag_in[0, 0:1, :LANES] == 0, 1.0, 0.0), (cap, LANES))
    x, y = sums_out[0].astype(jnp.float32), sums_out[1].astype(jnp.float32)
    held_rows = sums_answer.shape[1]
    unit = jnp.where(
        row_iota(held_rows, LANES) == lane_iota(held_rows, LANES), 1.0, 0.0
    ).astype(jnp.bfloat16)
    for d, chosen in enumerate((jnp.where(first > 0.5, x, y), jnp.where(first > 0.5, y, x))):
        sums_answer[d] = lax.dot_general(
            unit,
            chosen.astype(jnp.bfloat16),
            (((1,), (1,)), ((), ())),
            preferred_element_type=jnp.float32,
        ).astype(jnp.bfloat16)
    tag_out[...] = tag_in[0, :, :LANES]
    backs = [to_side(12, sums_answer, sums_back, d, forth=False) for d in range(2)]
    backs += [to_side(10, answer, back, d, forth=False) for d in range(2)]
    for copy in backs:
        copy.start()
    for copy in backs:
        copy.wait_send()
    for copy in (
        [store_to(6, key_out, got_keys, d, late) for d in range(2)]
        + [store_to(8, value_out, got_values, d, pl.ds(0, cap)) for d in range(2)]
    ):
        copy.start()
        stores.append(copy)
    for copy in backs:
        copy.wait_recv()

    def merge(base):
        at_rows = pl.ds(pl.multiple_of(base, span), span)
        row, column = base + row_iota(span, cap), lane_iota(span, cap)
        spread = []
        for d in range(2):
            hit = (row - start[d] == column) & (column < length[d])
            spread.append(jnp.where(hit, 1.0, 0.0).astype(jnp.bfloat16))

        def placed(a, b):
            return jnp.dot(
                spread[0], back[0, :, a:b], preferred_element_type=jnp.float32
            ) + jnp.dot(spread[1], back[1, :, a:b], preferred_element_type=jnp.float32)

        stat = sum(
            lax.dot_general(
                spread[d],
                sums_back[d],
                (((1,), (1,)), ((), ())),
                preferred_element_type=jnp.float32,
            )
            for d in range(2)
        )
        mine = logs[at_rows, :]
        has = base + row_iota(span, 1) < starts[2]
        own_part, prior_part = [], []
        for head in range(feat // HD):
            far = stat[:, 3 * head : 3 * head + 1]
            far = far + stat[:, 3 * head + 1 : 3 * head + 2]
            far = far + stat[:, 3 * head + 2 : 3 * head + 3]
            near = mine[:, head : head + 1]
            top = jnp.maximum(near, far)
            x, y = jnp.exp(near - top), jnp.exp(far - top)
            own_part.append(jnp.where(has, x / (x + y), 1.0))
            prior_part.append(jnp.where(has, y / (x + y), 0.0))
        lanes = lane_iota(span, LANES)
        for pair in range(feat // 256):
            both = placed(pair * 256, pair * 256 + 256)
            for side in range(2):
                a = pair * 256 + side * LANES
                b = a + LANES
                h0, h1 = a // HD, (b - 1) // HD
                x, y = own_part[h0], prior_part[h0]
                if h1 != h0:
                    x = jnp.where(lanes < h1 * HD - a, x, own_part[h1])
                    y = jnp.where(lanes < h1 * HD - a, y, prior_part[h1])
                far = both[:, side * LANES : side * LANES + LANES]
                total = own[at_rows, a:b].astype(jnp.float32) * x + far * y
                held[:, a:b] = total.astype(jnp.bfloat16)

    def project(target):
        def step(n, carry):
            at = pl.ds(pl.multiple_of(n * 512, 512), 512)
            target[:, at] = jnp.dot(
                held[...], weight[:, at], preferred_element_type=jnp.float32
            ).astype(target.dtype)
            return carry

        lax.fori_loop(0, weight.shape[1] // 512, step, 0)

    def chunk_of(n):
        return pl.ds(pl.multiple_of(n * chunk, chunk), chunk)

    locals_[5].wait()
    overs = []
    for n in range(chips - 1):
        merge(others[n] * span)
        project(part_a.at[n])
        near = remote(
            15 + n, part_a.at[n, chunk_of(1 - core), :], near_a.at[n], {"tp": sibling}
        )
        near.start()
        near.wait()
        far_send[n] = (
            part_a[n, chunk_of(core), :].astype(jnp.float32) + near_a[n].astype(jnp.float32)
        ).astype(far_send.dtype)
        overs.append(
            remote(14 + chips + n, far_send.at[n], far_in.at[n], {"tp": across[n]})
        )
        overs[n].start()
    merge(chip * span)
    project(part_b)
    last = remote(14, part_b.at[chunk_of(1 - core), :], near_b, {"tp": sibling})
    last.start()
    last.wait()
    total = part_b[chunk_of(core), :].astype(jnp.float32) + near_b[...].astype(jnp.float32)
    for n in range(chips - 1):
        overs[n].wait()
        total = total + far_in[n].astype(jnp.float32)
    mixed_ref[...] = total.astype(mixed_ref.dtype)
    for copy in stores:
        copy.wait()


def body(
    queries,
    keys_new,
    values_new,
    cache_keys,
    cache_values,
    out_proj,
    req_lengths,
    cache_owner,
    cache_slot,
    prior_len,
):
    rows, feat = queries.shape
    width = out_proj.shape[1]
    slots, prior = cache_keys.shape[:2]
    chips = lax.axis_size("tp") // 2
    span = rows // chips
    chunk = span // 2
    bf16 = jnp.bfloat16
    packed = (2, NEWCAP, feat)
    sums = (2, -(-3 * (feat // HD) // 16) * 16, NEWCAP)
    smem = pl.BlockSpec(memory_space=pltpu.SMEM)
    hbm = pl.BlockSpec(memory_space=pl.ANY)
    vmem = pl.BlockSpec(memory_space=pltpu.VMEM)
    mixed, key_first, key_second, value_first, value_second, tag = pl.pallas_call(
        functools.partial(whole_kernel, lax.axis_size("req"), chips),
        in_specs=[smem] * 4 + [hbm] * 6,
        out_specs=[vmem, hbm, hbm, hbm, hbm, vmem],
        out_shape=[
            jax.ShapeDtypeStruct((chunk, width), bf16),
            jax.ShapeDtypeStruct(packed[1:], bf16),
            jax.ShapeDtypeStruct(packed[1:], bf16),
            jax.ShapeDtypeStruct(packed[1:], bf16),
            jax.ShapeDtypeStruct(packed[1:], bf16),
            jax.ShapeDtypeStruct((8, LANES), jnp.int32),
        ],
        scratch_shapes=[
            pltpu.VMEM((rows, feat), bf16),
            pltpu.VMEM((rows, feat), bf16),
            pltpu.VMEM((rows, feat), bf16),
            pltpu.VMEM(cache_keys.shape, bf16),
            pltpu.VMEM(cache_values.shape, bf16),
            pltpu.VMEM(out_proj.shape, bf16),
            pltpu.VMEM(packed, bf16),
            pltpu.VMEM(packed, bf16),
            pltpu.VMEM(packed, bf16),
            pltpu.VMEM(packed, bf16),
            pltpu.VMEM((2, 8, prior), jnp.int32),
            pltpu.VMEM((2, 8, prior), jnp.int32),
            pltpu.VMEM(packed, bf16),
            pltpu.VMEM((2, NEWCAP, LANES), bf16),
            pltpu.VMEM(packed, bf16),
            pltpu.VMEM(packed, bf16),
            pltpu.VMEM(sums, bf16),
            pltpu.VMEM(sums, bf16),
            pltpu.VMEM((rows, feat), bf16),
            pltpu.VMEM((rows, LANES), jnp.float32),
            pltpu.VMEM((span, feat), bf16),
            pltpu.VMEM((chips - 1, span, width), bf16),
            pltpu.VMEM((span, width), bf16),
            pltpu.VMEM((chips - 1, chunk, width), bf16),
            pltpu.VMEM((chunk, width), bf16),
            pltpu.VMEM((chips - 1, chunk, width), bf16),
            pltpu.VMEM((chips - 1, chunk, width), bf16),
            pltpu.SemaphoreType.DMA((6,)),
            pltpu.SemaphoreType.DMA((13 + 2 * chips,)),
            pltpu.SemaphoreType.DMA((13 + 2 * chips,)),
        ],
        compiler_params=pltpu.CompilerParams(
            collective_id=0, has_side_effects=True, vmem_limit_bytes=VMEM_LIMIT
        ),
        cost_estimate=pl.CostEstimate(
            flops=2 * rows * feat * width, bytes_accessed=37_000_000, transcendentals=5_000_000
        ),
        name="whole",
    )(
        req_lengths, cache_owner, cache_slot, prior_len,
        queries, keys_new, values_new, cache_keys, cache_values, out_proj,
    )
    slot_ids = jnp.arange(slots, dtype=jnp.int32)[:, None, None]
    first = slot_ids == tag[0, 0]
    new_keys = jnp.where(first, key_first[None], key_second[None])
    new_values = jnp.where(first, value_first[None], value_second[None])
    return (mixed, new_keys, new_values)


def solution(mesh):
    in_specs = (
        P("req", "tp"),
        P("req", "tp"),
        P("req", "tp"),
        P("req", None, "tp"),
        P("req", None, "tp"),
        P("tp", None),
        P("req", None),
        P("req", None),
        P("req", None),
        P("req", None),
    )
    out_specs = (P(("req", "tp"), None), P("req", None, "tp"), P("req", None, "tp"))
    return jax.shard_map(body, mesh=mesh, in_specs=in_specs, out_specs=out_specs, check_vma=False)
```
